32 devices in a mesh: expert: 8 (over z, x), shard: 4 (over y, core).
Axes of the slice: x: 2, y: 2, z: 4, core: 2. Of those that a mesh axis runs over, the one named last changes fastest.
Arguments:
- inputs: float32 [8, 1024, 2048], P('expert', 'shard'), may hold values from -6 to 6
- segment_ids: int32 [8, 1024], P('expert'), may hold values from -1 to 1, as said below
- route_ids: int32 [8, 1024, 8], P('expert', 'shard'), may hold values from 0 to 31, all different within a row; in each aligned block of 256 rows (0 to 255, 256 to 511, ..., all dimensions but the last counted through in order) at most 64 rows name the same one
- norm_gains: float32 [4, 2048], P(None, ('expert', 'shard')), may hold values from 0.5 to 1.5
- w_query: float32 [2048, 2048], P(('expert', 'shard')), may hold values from -0.125 to 0.125
- w_key: float32 [2048, 2048], P(('expert', 'shard')), may hold values from -0.125 to 0.125
- w_value: float32 [2048, 2048], P(('expert', 'shard')), may hold values from -0.125 to 0.125
- w_output: float32 [2048, 2048], P(('expert', 'shard')), may hold values from -1 to 1
- w_router: float32 [2048, 32], P(('expert', 'shard')), may hold values from -0.0625 to 0.0625
- experts_gate: float32 [32, 2048, 1024], P('expert', 'shard'), may hold values from -0.125 to 0.125
- experts_up: float32 [32, 2048, 1024], P('expert', 'shard'), may hold values from -0.125 to 0.125
- experts_down: float32 [32, 1024, 2048], P('expert', 'shard'), may hold values from -6 to 6
- cotangent: float32 [8, 1024, 2048], P('expert', 'shard'), may hold values from -6 to 6
Outputs:
- output: float32 [8, 1024, 2048], P('expert', 'shard')
- grad_input: float32 [8, 1024, 2048], P('expert', 'shard')
- grad_gains: float32 [4, 2048], P(None, ('expert', 'shard'))
- grad_query: float32 [2048, 2048], P(('expert', 'shard'))
- grad_key: float32 [2048, 2048], P(('expert', 'shard'))
- grad_value: float32 [2048, 2048], P(('expert', 'shard'))
- grad_output: float32 [2048, 2048], P(('expert', 'shard'))
- grad_router: float32 [2048, 32], P(('expert', 'shard'))
- grad_experts_gate: float32 [32, 2048, 1024], P('expert', 'shard')
- grad_experts_up: float32 [32, 2048, 1024], P('expert', 'shard')
- grad_experts_down: float32 [32, 1024, 2048], P('expert', 'shard')
The draws below stay inside these ranges and needn't reach their ends.
Inputs may be any that keep to these rules, and one draw needn't show every extreme that they name: `segment_ids`: in each sequence, the tokens 2 j * 256 to (2 j + 2) * 256 - 1 hold exactly one picture piece of 256 consecutive tokens, all with the id j; every other token is text, with the id -1. `route_ids`: each token names 8 different experts. Among the 256 tokens of one device (aligned blocks of 256 tokens) no expert is named more than 64 times, a bound that some block reaches.
All inputs are finite; a program needn't handle non-finite values.
Results may differ from the reference program's by a relative error of at most 0.02.
Values may be sent and summed in bfloat16 or wider, within the bound.
No kernel may reach another device: no remote copies, remote signals or barrier semaphores. Data moves between devices by JAX's collectives and lax.ppermute only.
A program may use at most 448 MiB of HBM per device.

```python
import math
import jax
import jax.numpy as jnp
import numpy as np
from jax import lax

D = 2048
HEADS = 16
HEAD_DIM = 128
FF = 1024
TOP = 8
SEQ = 1024
PIECE = 256
EXPERTS = 32
SEQS = 8
TOK_DEV = 256
CAP = 64
N_SHARD = 4


def draw_segment_ids(key, part):
    key = jax.random.fold_in(key, 11)
    piece_count = SEQ // (2 * PIECE)
    offsets = jax.random.randint(key, (SEQS, piece_count), 0, PIECE + 1)
    positions = jnp.arange(SEQ, dtype=jnp.int32)
    slot_of = positions // (2 * PIECE)
    within = positions % (2 * PIECE)
    starts = offsets[:, slot_of]
    inside = (within[None, :] >= starts) & (within[None, :] < starts + PIECE)
    return jnp.where(inside, slot_of[None, :], -1).astype(jnp.int32)


def block_levels(stream_key, shape, split, low, high):
    def one(position, parts):
        draws = jax.random.uniform(jax.random.fold_in(jax.random.fold_in(stream_key, 6), position), (parts,), jnp.float32, low / len(split), high / len(split))
        return jnp.repeat(jnp.exp(draws), shape[position] // parts).reshape((-1,) + (1,) * (len(shape) - position - 1))

    loudness = one(*split[0])
    for cut in split[1:]:
        loudness = loudness * one(*cut)
    return loudness


def shared_out(stream_key, own, number, rows, number_of, top, most, slope):
    sequence = jax.random.permutation(stream_key, number_of)
    heavy_load, common = shares(number_of, rows * top, most, slope, True), shares(number_of, rows * top, most, slope, False)
    places = jnp.arange(number_of)

    def named(sizes, offset_by):
        used = int((sizes > 0).sum())
        fixed = max(1, used // 4)
        shifted = fixed + (places - fixed + offset_by * (used - fixed)) % max(1, number_of - fixed)
        return jnp.zeros((number_of,), jnp.int32).at[sequence[jnp.where(places < fixed, places, shifted)]].set(jnp.asarray(sizes, jnp.int32))

    sizes = jnp.where(number % 4 == 0, named(heavy_load, number // 4), named(common, number - number // 4 - 1))
    mixed = jax.random.permutation(jax.random.fold_in(own, 3), number_of)
    donor, taker = mixed[0:number_of // 2 * 2:2], mixed[1:number_of // 2 * 2:2]
    room = jnp.minimum(sizes[donor] - 1, most - sizes[taker]) // 2
    room = jnp.where((donor == sequence[0]) | (taker == sequence[0]) | (sizes[taker] == 0), 0, jnp.maximum(room, 0))
    shifted = jax.random.randint(jax.random.fold_in(own, 4), (number_of // 2,), 0, 1 << 20) % (room + 1)
    sizes = sizes.at[donor].add(-shifted).at[taker].add(shifted)
    items = jnp.searchsorted(jnp.cumsum(sizes), jnp.arange(rows * top), side="right").astype(jnp.int32)
    table = items.reshape(top, rows).T
    table = table[jax.random.permutation(jax.random.fold_in(own, 1), rows)]
    offset_by = jax.random.randint(jax.random.fold_in(own, 2), (rows, 1), 0, top)
    return jnp.take_along_axis(table, (jnp.arange(top)[None, :] + offset_by) % top, axis=1)


def shares(amount, total, most, skew, full):
    loads = [(1 << 20) // math.isqrt(grade ** skew) + 1 for grade in range(1, amount + 1)]
    largest = most if full else min(most, max(-(-total // amount), total * loads[0] // sum(loads)))
    least = 1 if total - largest >= amount - 1 else 0
    given, rest = [largest] + [least] * (amount - 1), total - largest - least * (amount - 1)
    while rest > 0:
        candidates = [i for i in range(1, amount) if given[i] < largest] or [i for i in range(1, amount) if given[i] < most]
        mass, left = sum([loads[i] for i in candidates]), rest
        for i in candidates:
            more = min(most - given[i], max(1, left * loads[i] // mass), rest)
            given[i] = given[i] + more
            rest = rest - more
    return np.array(given)


def noise(rng, dims, spread, limit, split=(), kind=jnp.bfloat16):
    drawn = jax.random.normal(rng, dims, jnp.float32) * spread
    if len(split) > 0:
        drawn = block_levels(rng, dims, split, -0.22, 0.18) * drawn
    return jnp.clip(drawn, min=-limit, max=limit).astype(kind)


def setup_inputs(seed: int = 0) -> dict:
    streams_of = jax.random.split(jax.random.key(seed), 14)
    inputs = noise(streams_of[0], (SEQS, SEQ, D), 1.0, 6.0, ((0, 8), (1, 4)), jnp.float32)
    segment_ids = draw_segment_ids(jax.random.fold_in(streams_of[13], 71), 0)
    route_ids_keys = jax.random.split(jax.random.fold_in(streams_of[2], 1), SEQS * SEQ // TOK_DEV)
    route_ids_turns = jax.random.permutation(jax.random.fold_in(streams_of[2], 3), SEQS * SEQ // TOK_DEV)
    route_ids = jax.vmap(lambda own, number: shared_out(jax.random.fold_in(streams_of[2], 2), own, number, TOK_DEV, EXPERTS, TOP, CAP, 2))(route_ids_keys, route_ids_turns).reshape((SEQS, SEQ, TOP))
    norm_gains = jnp.clip(1.0 + 0.1 * jax.random.normal(streams_of[3], (4, D), jnp.float32), 0.5, 1.5)
    w_query = noise(streams_of[4], (D, D), D ** -0.5, 0.125, ((0, 32),), jnp.float32)
    w_key = noise(streams_of[5], (D, D), D ** -0.5, 0.125, ((0, 32),), jnp.float32)
    w_value = noise(streams_of[6], (D, D), D ** -0.5, 0.125, ((0, 32),), jnp.float32)
    w_output = noise(streams_of[7], (D, D), (max(D // 64, 1)) ** -0.5, 1.0, ((0, 32),), jnp.float32)
    w_router = noise(streams_of[8], (D, EXPERTS), (4 * D) ** -0.5, 0.0625, ((0, 32),), jnp.float32)
    experts_gate = noise(streams_of[9], (EXPERTS, D, FF), D ** -0.5, 0.125, ((0, 8), (1, 4)), jnp.float32)
    experts_up = noise(streams_of[10], (EXPERTS, D, FF), D ** -0.5, 0.125, ((0, 8), (1, 4)), jnp.float32)
    experts_down = noise(streams_of[11], (EXPERTS, FF, D), 1 ** -0.5, 6.0, ((0, 8), (1, 4)), jnp.float32)
    cotangent = noise(streams_of[12], (SEQS, SEQ, D), 1.0, 6.0, ((0, 8), (1, 4)), jnp.float32)
    return {"inputs": inputs, "segment_ids": segment_ids, "route_ids": route_ids, "norm_gains": norm_gains, "w_query": w_query, "w_key": w_key, "w_value": w_value, "w_output": w_output, "w_router": w_router, "experts_gate": experts_gate, "experts_up": experts_up, "experts_down": experts_down, "cotangent": cotangent}


EPSILON = 1e-05
ROPE_BASE = 10000.0

@jax.custom_vjp
def low(v):
    return lax.optimization_barrier(v.astype(jnp.bfloat16)).astype(jnp.float32)

@jax.custom_vjp
def low_back(v):
    return v

def low_keep(v):
    return (low(v), None)

def low_pass(kept, grad):
    return (grad,)

def back_keep(v):
    return (v, None)

def back_low(kept, grad):
    return (low(grad),)
low.defvjp(low_keep, low_pass)
low_back.defvjp(back_keep, back_low)

def rms_norm(values, gain_row):
    return values * lax.rsqrt(lax.optimization_barrier(jnp.mean(values * values, axis=-1, keepdims=True)) + EPSILON) * gain_row

def rotate(values, positions):
    half_dim = values.shape[-1] // 2
    frequency = ROPE_BASE ** (-2.0 * jnp.arange(half_dim, dtype=jnp.float32) / values.shape[-1])
    angles = positions.astype(jnp.float32)[:, None] * frequency[None, :]
    cosine = jnp.cos(angles)[:, None, :]
    sine_part = jnp.sin(angles)[:, None, :]
    first_half = values[..., :half_dim]
    second = values[..., half_dim:]
    return jnp.concatenate([first_half * cosine - second * sine_part, second * cosine + first_half * sine_part], axis=-1)

def head_norm(raw_rows, gain_row, positions):
    normed_rows = rms_norm(raw_rows, gain_row)
    return rotate(normed_rows.reshape(raw_rows.shape[0], HEADS, HEAD_DIM), positions)

def one_sequence(token_rows, segments, routes, weights):
    gain_low, weight_query, weight_key, weight_value, weight_output, weight_router, gate_low, up_low, down_low = weights
    highest = lax.Precision.HIGHEST
    positions = jnp.arange(SEQ, dtype=jnp.int32)
    normed = low(rms_norm(token_rows, gain_low[0]))
    query_raw = low_back(jnp.dot(normed, weight_query, precision=highest))
    key_raw = low_back(jnp.dot(normed, weight_key, precision=highest))
    value_rows = low_back(low(jnp.dot(normed, weight_value, precision=highest)))
    query_heads = low_back(low(head_norm(query_raw, gain_low[1], positions)))
    key_heads = low_back(low(head_norm(key_raw, gain_low[2], positions)))
    value_heads = value_rows.reshape(SEQ, HEADS, HEAD_DIM)
    allowed = (positions[None, :] <= positions[:, None]) | (segments[:, None] == segments[None, :]) & (segments[:, None] >= 0)
    scores = low_back(jnp.einsum('qhd,khd->hqk', query_heads, key_heads, precision=highest) * HEAD_DIM ** (-0.5))
    probs = low(jax.nn.softmax(jnp.where(allowed[None], scores, -jnp.inf), axis=-1))
    attended = low_back(low(jnp.einsum('hqk,khd->qhd', probs, value_heads, precision=highest))).reshape(SEQ, D)
    hidden = token_rows + low_back(jnp.dot(attended, weight_output, precision=highest))
    mlp_in = low(rms_norm(hidden, gain_low[3]))
    logits = low_back(jnp.dot(mlp_in, weight_router, precision=highest))
    router = jax.nn.softmax(logits, axis=-1)
    gate_values = jnp.take_along_axis(router, routes, axis=1)
    pair_rows = low_back(jnp.repeat(mlp_in, TOP, axis=0))
    pair_ids = routes.reshape(-1)
    sorted_pairs = jnp.argsort(pair_ids, stable=True).astype(jnp.int32)
    expert_range = jnp.arange(EXPERTS, dtype=jnp.int32)
    counts = lax.optimization_barrier(jnp.sum((pair_ids[:, None] == expert_range[None, :]).astype(jnp.int32), axis=0))
    starts = jnp.cumsum(counts) - counts
    rank_index = jnp.arange(N_SHARD * CAP, dtype=jnp.int32)
    is_valid = (rank_index[None, :] < counts[:, None]).astype(jnp.float32)[:, :, None]
    row_table = sorted_pairs[jnp.minimum(starts[:, None] + rank_index[None, :], SEQ * TOP - 1)]
    expert_in = pair_rows[row_table] * is_valid
    gate_pre = low_back(jnp.einsum('erd,edf->erf', expert_in, gate_low, precision=highest))
    up_pre = low_back(jnp.einsum('erd,edf->erf', expert_in, up_low, precision=highest))
    activation = low(jax.nn.silu(gate_pre) * up_pre)
    expert_out = low(jnp.einsum('erf,efd->erd', activation, down_low, precision=highest))
    pair_out = low_back(jnp.zeros((SEQ * TOP, D), jnp.float32).at[row_table].add(expert_out * is_valid))
    mixture = lax.optimization_barrier(jnp.sum(gate_values[:, :, None] * pair_out.reshape(SEQ, TOP, D), axis=1))
    return hidden + mixture

def layer_forward(inputs, norm_gains, w_query, w_key, w_value, w_output, w_router, experts_gate, experts_up, experts_down, segment_ids, route_ids):
    weights = (low(norm_gains), low(w_query), low(w_key), low(w_value), low(w_output), low(w_router), low(experts_gate), low(experts_up), low(experts_down))

    def sequence_step(items):
        return one_sequence(items[0], items[1], items[2], weights)
    return lax.map(jax.checkpoint(sequence_step), (inputs, segment_ids, route_ids))

def reference(inputs, segment_ids, route_ids, norm_gains, w_query, w_key, w_value, w_output, w_router, experts_gate, experts_up, experts_down, cotangent):

    def forward(inputs_f, gains_f, query_f, key_f, value_f, output_f, router_f, gate_f, up_f, down_f):
        return layer_forward(inputs_f, gains_f, query_f, key_f, value_f, output_f, router_f, gate_f, up_f, down_f, segment_ids, route_ids)
    output, pull_back = jax.vjp(forward, inputs, norm_gains, w_query, w_key, w_value, w_output, w_router, experts_gate, experts_up, experts_down)
    grads = pull_back(cotangent)
    return (output, grads[0], grads[1], grads[2], grads[3], grads[4], grads[5], grads[6], grads[7], grads[8], grads[9])
```

```python
from functools import partial

import jax
import jax.numpy as jnp
from jax import lax
from jax.experimental import pallas as pl
from jax.experimental.pallas import tpu as pltpu
from jax.sharding import PartitionSpec as P

HEAD_DIM = 128
EXP_DEV = 4
BLOCK = 512
EPSILON = 1e-05
ROPE_BASE = 10000.0
LOW = jnp.bfloat16
F32 = jnp.float32


def inverse_rms(mean_square):
    return lax.rsqrt(mean_square + EPSILON)


def rms_back(values, inverse, gain, grad):
    scaled = gain * grad
    inner = jnp.mean(values * scaled, axis=-1, keepdims=True)
    values_grad = inverse * scaled - values * (inverse * inverse * inverse * inner)
    gain_grad = jnp.sum(grad * values * inverse, axis=0)
    return values_grad, gain_grad


def mm(left, right):
    return jnp.dot(left, right, preferred_element_type=F32)


def dot_last(left, right):
    return lax.dot_general(left, right, (((1,), (1,)), ((), ())), preferred_element_type=F32)


def dot_first(left, right):
    return lax.dot_general(left, right, (((0,), (0,)), ((), ())), preferred_element_type=F32)


def rope_tables(count):
    half = HEAD_DIM // 2
    frequency = ROPE_BASE ** (-2.0 * jnp.arange(half, dtype=F32) / HEAD_DIM)
    angles = jnp.arange(count, dtype=F32)[:, None] * frequency[None, :]
    cosine = jnp.cos(angles)
    sine = jnp.sin(angles)
    return (
        jnp.concatenate([cosine, cosine], axis=-1),
        jnp.concatenate([-sine, sine], axis=-1),
    )


def ring_order(ways):
    return list(range(0, ways, 2)) + list(range(1, ways, 2))[::-1]


def ring_order_inverse(ways):
    order = ring_order(ways)
    return [order.index(i) for i in range(ways)]


def ring_steps(ways):
    order = ring_order(ways)
    forward = [(order[i], order[(i + 1) % ways]) for i in range(ways)]
    return forward, [(b, a) for a, b in forward]


def tie(value, others):
    value, others = lax.optimization_barrier((value, others))
    return value, others


class RingGather:
    def __init__(self, block, ways):
        self.ways, self.done = ways, 0
        self.forward, self.backward = ring_steps(ways)
        self.held = {0: block}

    def step(self):
        ways, far = self.ways, self.ways // 2
        self.done += 1
        step = self.done
        held = self.held
        held[step] = lax.ppermute(held[step - 1], "expert", self.forward)
        if step < ways - far:
            before = held[(ways - step + 1) % ways]
            held[ways - step] = lax.ppermute(before, "expert", self.backward)

    def finish(self):
        while self.done < self.ways // 2:
            self.step()
        return [self.held[i] for i in range(self.ways)]

    def tie(self, value):
        value, self.held = tie(value, self.held)
        return value

    def last(self):
        return self.held[self.done]


class RingScatter:
    def __init__(self, piece, ways):
        self.piece, self.ways = piece, ways
        self.forward, self.backward = ring_steps(ways)
        self.far = ways // 2
        self.near = ways - 1 - self.far
        self.left_step, self.right_step = self.near, self.far
        self.state = (piece(ways - self.far), piece(self.near))

    def add(self, got, index):
        return (got.astype(F32) + self.piece(index).astype(F32)).astype(LOW)

    def step(self):
        right, left = self.state
        if self.right_step == self.left_step:
            left = lax.ppermute(left, "expert", self.backward)
            self.left_step -= 1
            if self.left_step:
                left = self.add(left, self.left_step)
        right = lax.ppermute(right, "expert", self.forward)
        self.right_step -= 1
        if self.right_step:
            right = self.add(right, self.ways - self.right_step)
        self.state = (right, left)

    def finish(self):
        while self.right_step:
            self.step()
        right, left = self.state
        return self.piece(0).astype(F32) + right.astype(F32) + left.astype(F32)

    def tie(self, value):
        value, self.state = tie(value, self.state)
        return value


def flip_steps(shards, distance):
    return [(i, i ^ distance) for i in range(shards)]


class ShardGather:
    def __init__(self, block, shards):
        self.shards, self.distance = shards, shards // 2
        self.held = {0: block}

    def hop(self):
        steps = flip_steps(self.shards, self.distance)
        for key in list(self.held):
            self.held[key ^ self.distance] = lax.ppermute(self.held[key], "shard", steps)
        self.distance //= 2

    def tie(self, value):
        value, self.held = tie(value, self.held)
        return value

    def whole(self, mine):
        while self.distance:
            self.hop()
        size = self.held[0].shape[0]
        shape = (self.shards * size,) + self.held[0].shape[1:]
        whole = jnp.zeros(shape, self.held[0].dtype)
        for key, piece in self.held.items():
            whole = lax.dynamic_update_slice_in_dim(whole, piece, (mine ^ key) * size, 0)
        return whole


class ShardScatter:
    def __init__(self, pieces, shards):
        self.shards, self.distance = shards, 1
        self.held = dict(enumerate(pieces))

    def hop(self, late=None):
        steps = flip_steps(self.shards, self.distance)
        last = 2 * self.distance == self.shards
        for key in list(self.held):
            if key & self.distance:
                got = lax.ppermute(self.held.pop(key), "shard", steps)
                if late is not None:
                    got, _ = tie(got, late)
                rest = self.held[key ^ self.distance].astype(F32) + got.astype(F32)
                self.held[key ^ self.distance] = rest if last else rest.astype(LOW)
        self.distance *= 2

    def finish(self):
        while self.distance < self.shards:
            self.hop()
        return self.held[0]


def shard_pieces(whole, shards, mine):
    size = whole.shape[0] // shards
    return [
        lax.dynamic_slice_in_dim(whole, (mine ^ key) * size, size, 0) for key in range(shards)
    ]


def dispatch_body(ways, *refs):
    pick_ref, sources, out_ref = refs[0], refs[1:-1], refs[-1]
    experts, _, capacity, tokens = pick_ref.shape
    for block in range(ways):
        pick = pick_ref[:, block].reshape(experts * capacity, tokens)
        got = mm(pick, sources[block][...]).astype(LOW)
        out_ref[:, block * capacity : (block + 1) * capacity, :] = got.reshape(
            experts, capacity, got.shape[-1]
        )


def dispatch(pick, blocks):
    experts, ways, capacity, tokens = pick.shape
    width = blocks[0].shape[-1]
    chunk = 512
    return pl.pallas_call(
        partial(dispatch_body, ways),
        grid=(width // chunk,),
        in_specs=[pl.BlockSpec(pick.shape, lambda i: (0, 0, 0, 0))]
        + [pl.BlockSpec((tokens, chunk), lambda i: (0, i))] * ways,
        out_specs=pl.BlockSpec((experts, ways * capacity, chunk), lambda i: (0, 0, i)),
        out_shape=jax.ShapeDtypeStruct((experts, ways * capacity, width), LOW),
        compiler_params=pltpu.CompilerParams(vmem_limit_bytes=48 * 2**20),
        cost_estimate=pl.CostEstimate(
            flops=2 * experts * ways * capacity * tokens * width,
            bytes_accessed=4 * experts * ways * capacity * width,
            transcendentals=0,
        ),
        name="dispatch",
    )(pick, *blocks)


def expert_body(
    places_ref, rows_ref, grads_ref, router_ref, gate, up, down,
    act_ref, gate_out, up_out, pair_ref, weighted_ref, slot_ref,
):
    expert = places_ref[0] * EXP_DEV + pl.program_id(0)
    rows = rows_ref[0]
    logits = mm(rows, router_ref[...])
    logits = jnp.exp(logits - jnp.max(logits, axis=-1, keepdims=True))
    mine = lax.broadcasted_iota(jnp.int32, logits.shape, 1) == expert
    slot_gate = jnp.sum(jnp.where(mine, logits, 0.0), axis=-1, keepdims=True) / jnp.sum(
        logits, axis=-1, keepdims=True
    )
    gate_pre, up_pre = mm(rows, gate[0]), mm(rows, up[0])
    grads = grads_ref[0].astype(F32)
    pair_ref[0] = (slot_gate * grads).astype(LOW)
    sig = 1.0 / (1.0 + jnp.exp(-gate_pre))
    silu = gate_pre * sig
    act_ref[0] = (silu * up_pre).astype(LOW)
    act_grad = dot_last(pair_ref[0], down[0])
    gate_out[0] = (act_grad * up_pre * (sig + silu * (1.0 - sig))).astype(LOW)
    up_out[0] = (act_grad * silu).astype(LOW)
    pair_out = mm(act_ref[0], down[0])
    slot_ref[0] = jnp.sum(pair_out * grads, axis=-1, keepdims=True)
    weighted_ref[0] = (slot_gate * pair_out).astype(LOW)


def row_grad_body(gate_ref, up_ref, gate, up, back_ref):
    back = dot_last(gate_ref[0], gate[0]) + dot_last(up_ref[0], up[0])
    back_ref[0] = back.astype(LOW)


def expert_block(chunk, size):
    return pl.BlockSpec((1, chunk, size), lambda e, r, *p: (e, r, 0))


def expert_weight(array):
    return pl.BlockSpec((1,) + array.shape[1:], lambda e, r, *p: (e, 0, 0))


def expert_cost(experts, total, width, hidden, products):
    return pl.CostEstimate(
        flops=2 * products * experts * total * width * hidden,
        bytes_accessed=2 * experts * (4 * total * width + 3 * hidden * (total + width)),
        transcendentals=experts * total * hidden,
    )


def expert_pass(places, rows, grads, router, gate, up, down):
    experts, total, width = rows.shape
    hidden = gate.shape[-1]
    chunk = min(256, total)
    sizes = [hidden, hidden, hidden, width, width]
    return pl.pallas_call(
        expert_body,
        grid_spec=pltpu.PrefetchScalarGridSpec(
            num_scalar_prefetch=1,
            grid=(experts, total // chunk),
            in_specs=[expert_block(chunk, width)] * 2
            + [pl.BlockSpec(router.shape, lambda e, r, p: (0, 0))]
            + [expert_weight(w) for w in (gate, up, down)],
            out_specs=[expert_block(chunk, size) for size in sizes + [1]],
        ),
        out_shape=[jax.ShapeDtypeStruct((experts, total, size), LOW) for size in sizes]
        + [jax.ShapeDtypeStruct((experts, total, 1), F32)],
        compiler_params=pltpu.CompilerParams(vmem_limit_bytes=60 * 2**20),
        cost_estimate=expert_cost(experts, total, width, hidden, 4),
        name="experts",
    )(places, rows, grads, router, gate, up, down)


def row_grads(gate_grad, up_grad, gate, up):
    experts, total, hidden = gate_grad.shape
    width = gate.shape[1]
    chunk = total
    return pl.pallas_call(
        row_grad_body,
        grid=(experts, total // chunk),
        in_specs=[expert_block(chunk, hidden)] * 2 + [expert_weight(gate), expert_weight(up)],
        out_specs=expert_block(chunk, width),
        out_shape=jax.ShapeDtypeStruct((experts, total, width), LOW),
        compiler_params=pltpu.CompilerParams(vmem_limit_bytes=48 * 2**20),
        cost_estimate=expert_cost(experts, total, width, hidden, 2),
        name="row_grads",
    )(gate_grad, up_grad, gate, up)


def rope(values, cosine, sine):
    return values * cosine + pltpu.roll(values, HEAD_DIM // 2, 1) * sine


def rope_back(values, cosine, sine):
    return values * cosine - pltpu.roll(values, HEAD_DIM // 2, 1) * sine


def attend_body(
    query_raw, key_raw, value_raw, inverse, gain_query, gain_key, cosine, sine,
    segment_column, segment_row, query_ref, key_ref, value_ref, out_ref, total_ref,
):
    seq = query_raw.shape[0]
    block = min(BLOCK, seq)
    cos, sin = cosine[...], sine[...]
    query = query_raw[...] * inverse[:, 0:1] * gain_query[...]
    query_ref[...] = rope(query, cos, sin).astype(LOW)
    key = key_raw[...] * inverse[:, 1:2] * gain_key[...]
    key_ref[...] = rope(key, cos, sin).astype(LOW)
    value_ref[...] = value_raw[...].astype(LOW)
    for start in range(0, seq, block):
        stop = start + block
        at = slice(start, stop)
        scores = dot_last(query_ref[at], key_ref[:stop]) * HEAD_DIM ** (-0.5)
        row = lax.broadcasted_iota(jnp.int32, scores.shape, 0) + start
        column = lax.broadcasted_iota(jnp.int32, scores.shape, 1)
        own = segment_column[at]
        same = (own == segment_row[:, :stop]) & (own >= 0)
        scores = jnp.where((column <= row) | same, scores, -jnp.inf)
        top = jnp.max(scores, axis=-1, keepdims=True)
        probs = jnp.exp(scores - top)
        total = jnp.sum(probs, axis=-1, keepdims=True)
        probs = (probs * (1.0 / total)).astype(LOW)
        out_ref[at] = mm(probs, value_ref[:stop]).astype(LOW)
        total_ref[0, at] = top + jnp.log(total)


def attend_back_body(
    query_ref, key_ref, value_ref, grad_ref, total_ref, cosine, sine,
    segment_column, segment_row, query_out, key_out, value_out, key_sum, value_sum,
):
    seq = query_ref.shape[0]
    block = min(BLOCK, seq)
    cos, sin = cosine[...], sine[...]
    scale = HEAD_DIM ** (-0.5)
    key_sum[...] = jnp.zeros_like(key_sum)
    value_sum[...] = jnp.zeros_like(value_sum)
    for start in range(0, seq, block):
        stop = start + block
        at = slice(start, stop)
        query, grad = query_ref[at], grad_ref[at]
        scores = dot_last(key_ref[:stop], query) * scale
        row = lax.broadcasted_iota(jnp.int32, scores.shape, 0)
        column = lax.broadcasted_iota(jnp.int32, scores.shape, 1) + start
        own = segment_row[:, at]
        same = (segment_column[:stop] == own) & (own >= 0)
        allowed = (row <= column) | same
        probs = jnp.exp(jnp.where(allowed, scores - total_ref[0, :, at], -jnp.inf))
        probs_grad = dot_last(value_ref[:stop], grad)
        delta = jnp.sum(probs * probs_grad, axis=0, keepdims=True)
        score_grad = (probs * (probs_grad - delta)).astype(LOW)
        value_sum[:stop] += mm(probs.astype(LOW), grad)
        key_sum[:stop] += mm(score_grad, query)
        query_grad = (dot_first(score_grad, key_ref[:stop]) * scale).astype(LOW)
        query_out[at] = rope_back(query_grad.astype(F32), cos[at], sin[at])
    key_grad = (key_sum[...] * scale).astype(LOW)
    key_out[...] = rope_back(key_grad.astype(F32), cos, sin)
    value_out[...] = value_sum[...].astype(LOW)


def whole_block(array):
    return pl.BlockSpec(array.shape, lambda h: (0,) * array.ndim)


def head_block(rows, offset=0):
    return pl.BlockSpec((rows, HEAD_DIM), lambda h: (0, h + offset))


def attend_cost(heads, seq, products):
    return pl.CostEstimate(
        flops=products * 2 * heads * seq * seq * HEAD_DIM,
        bytes_accessed=heads * seq * HEAD_DIM * 24,
        transcendentals=heads * seq * seq,
    )


def attend(raw, inverse, gain_query, gain_key, cosine, sine, segments):
    seq = raw.shape[0]
    part = raw.shape[1] // 3
    heads = part // HEAD_DIM
    column, row = segments[:, None], segments[None, :]
    fixed = [cosine, sine, column, row]
    shape = jax.ShapeDtypeStruct((seq, part), LOW)
    return pl.pallas_call(
        attend_body,
        grid=(heads,),
        in_specs=[head_block(seq), head_block(seq, heads), head_block(seq, 2 * heads)]
        + [whole_block(inverse), head_block(1), head_block(1)]
        + [whole_block(array) for array in fixed],
        out_specs=[head_block(seq)] * 4 + [pl.BlockSpec((1, seq, 1), lambda h: (h, 0, 0))],
        out_shape=[shape] * 4 + [jax.ShapeDtypeStruct((heads, seq, 1), F32)],
        compiler_params=pltpu.CompilerParams(vmem_limit_bytes=48 * 2**20),
        cost_estimate=attend_cost(heads, seq, 2),
        name="attend",
    )(raw, raw, raw, inverse, gain_query[None], gain_key[None], *fixed)


def attend_back(query, key, value, grad, total, cosine, sine, segments):
    seq, part = query.shape
    heads = part // HEAD_DIM
    fixed = [cosine, sine, segments[:, None], segments[None, :]]

    def shape(kind):
        return jax.ShapeDtypeStruct((seq, part), kind)

    return pl.pallas_call(
        attend_back_body,
        grid=(heads,),
        in_specs=[head_block(seq)] * 4
        + [pl.BlockSpec((1, 1, seq), lambda h: (h, 0, 0))]
        + [whole_block(array) for array in fixed],
        out_specs=[head_block(seq)] * 3,
        out_shape=[shape(F32), shape(F32), shape(LOW)],
        scratch_shapes=[pltpu.VMEM((seq, HEAD_DIM), F32)] * 2,
        compiler_params=pltpu.CompilerParams(vmem_limit_bytes=48 * 2**20),
        cost_estimate=attend_cost(heads, seq, 5),
        name="attend_back",
    )(query, key, value, grad, total.reshape(heads, 1, seq), *fixed)


def tile_sum(values):
    tiles = lax.psum(values.reshape(-1, 128), "shard")
    return lax.optimization_barrier(tiles).reshape(values.shape)


def spread(block, axes, count):
    copies = jnp.broadcast_to(block[None], (count,) + block.shape)
    return lax.all_to_all(copies, axes, split_axis=0, concat_axis=0, tiled=True)


def per_device(
    inputs,
    segment_ids,
    route_ids,
    norm_gains,
    w_query,
    w_key,
    w_value,
    w_output,
    w_router,
    experts_gate,
    experts_up,
    experts_down,
    cotangent,
):
    rows = inputs[0]
    out_grad = cotangent[0]
    tokens, width = rows.shape
    capacity = tokens // 4
    ways = lax.axis_size("expert")
    shards = lax.axis_size("shard")
    both = ("expert", "shard")
    part = width // shards
    own_rows = w_query.shape[0]
    seq = tokens * shards
    my_expert = lax.axis_index("expert")
    my_shard = lax.axis_index("shard")
    devices = ways * shards
    to_slice = [(i, (i % ways) * shards + i // ways) for i in range(devices)]
    from_slice = [(b, a) for a, b in to_slice]

    three = jnp.stack([w_query, w_key, w_value], axis=1).astype(LOW)
    three = three.reshape(own_rows, 3, shards, part).transpose(2, 0, 1, 3)
    three = three.reshape(shards, own_rows, 3 * part)
    gate_low, three = tie(experts_gate.astype(LOW), three)
    grad_ring = RingGather(out_grad.astype(LOW), ways)
    grad_ring.step()
    mixed_three = jnp.zeros_like(three)
    for key in range(shards):
        other = my_shard ^ key
        piece = lax.dynamic_slice_in_dim(three, other, 1, 0)
        if key:
            piece = lax.ppermute(piece, "shard", flip_steps(shards, key))
        mixed_three = lax.dynamic_update_slice_in_dim(mixed_three, piece, other, 0)
    (experts_up, experts_down), three = tie((experts_up, experts_down), mixed_three)
    small = jnp.concatenate([norm_gains.T, w_router], axis=1).astype(LOW)
    small_all = spread(small, both, devices).reshape(width, -1)
    gains = small_all[:, :4].astype(F32).T
    weight_router = small_all[:, 4:]
    gain_attn, gain_mlp = gains[0], gains[3]
    gain_query = lax.dynamic_slice_in_dim(gains[1], my_shard * part, part)
    gain_key = lax.dynamic_slice_in_dim(gains[2], my_shard * part, part)

    my_place = jnp.array(ring_order_inverse(ways), jnp.int32)[my_expert]
    ring = jnp.array(ring_order(ways), jnp.int32)[(my_place - jnp.arange(ways)) % ways]
    slice_rows = shards * own_rows
    three_ring = RingGather(three.reshape(slice_rows, 3 * part), ways)
    inverse_rows = inverse_rms(jnp.mean(rows * rows, axis=-1, keepdims=True))
    normed = (rows * inverse_rows * gain_attn).astype(LOW)
    normed_ring = ShardGather(normed, shards)
    normed_ring.hop()
    moved_output = lax.ppermute(w_output.astype(LOW), both, to_slice)
    output_ring = RingGather(moved_output, ways)
    three_ring.step()
    three_ring.held = grad_ring.tie(three_ring.held)
    for _ in range(ways // 2 - 2):
        output_ring.step()
        three_ring.step()
        three_ring.held = output_ring.tie(three_ring.held)
    three_ring.held = normed_ring.tie(three_ring.held)
    output_ring.step()
    normed_all = normed_ring.whole(my_shard)
    weight_three = jnp.zeros((width, 3 * part), LOW)
    three_parts = three_ring.finish()
    output_parts = output_ring.finish()
    for step, piece in enumerate(three_parts):
        weight_three = lax.dynamic_update_slice_in_dim(
            weight_three, piece, ring[step] * slice_rows, 0
        )
    grad_ring.held, _ = tie(grad_ring.held, three_parts[ways // 2])
    raw = mm(normed_all, weight_three)
    query_raw, key_raw = raw[:, :part], raw[:, part : 2 * part]
    squares = jnp.stack(
        [jnp.sum(query_raw * query_raw, axis=-1), jnp.sum(key_raw * key_raw, axis=-1)]
    )
    squares = tile_sum(squares)
    inverse_qk = inverse_rms(squares / width)
    inverse_query, inverse_key = inverse_qk[0][:, None], inverse_qk[1][:, None]
    cosine, sine = rope_tables(seq)
    segments = segment_ids[0]
    query, key, value, attended, log_total = attend(
        raw, inverse_qk.T, gain_query, gain_key, cosine, sine, segments
    )
    grad_ring.step()
    attended = grad_ring.tie(attended)
    grad_ring.step()
    weight_output = jnp.zeros((own_rows * ways, width), LOW)
    for step, piece in enumerate(output_parts):
        weight_output = lax.dynamic_update_slice_in_dim(
            weight_output, piece, ring[step] * own_rows, 0
        )
    projected = mm(attended, weight_output).astype(LOW)
    projected = ShardScatter(shard_pieces(projected, shards, my_shard), shards)
    projected.hop()
    grad_ring.step()
    hidden = rows + projected.finish()
    inverse_hidden = inverse_rms(jnp.mean(hidden * hidden, axis=-1, keepdims=True))
    mlp_in = (hidden * inverse_hidden * gain_mlp).astype(LOW)

    routes_all = jnp.take(spread(route_ids[0].T, "expert", ways), ring, axis=0)
    mlp_in = grad_ring.tie(mlp_in)
    mlp_ring = RingGather(mlp_in, ways)
    mlp_ring.step()
    expert_names = my_expert * EXP_DEV + jnp.arange(EXP_DEV, dtype=jnp.int32)
    chosen = jnp.any(routes_all[None] == expert_names[:, None, None, None], axis=2)
    places = jnp.arange(tokens, dtype=jnp.int32)
    before = (places[:, None] < places[None, :]).astype(LOW)
    rank = jnp.einsum("lbt,tu->lbu", chosen.astype(LOW), before, preferred_element_type=F32)
    rank = jnp.where(chosen, rank.astype(jnp.int32), -1)
    slots = jnp.arange(capacity, dtype=jnp.int32)
    pick = rank[:, :, None, :] == slots[None, None, :, None]
    pick_low = pick.astype(LOW)

    weights_gate = lax.all_gather(gate_low, "shard", axis=1, tiled=True)
    weights_up = lax.all_gather(experts_up.astype(LOW), "shard", axis=1, tiled=True)
    weights_down = lax.all_gather(experts_down.astype(LOW), "shard", axis=1, tiled=True)

    logits = mm(mlp_in, weight_router)
    router = jax.nn.softmax(logits, axis=-1)

    def combine(values):
        return jnp.einsum(
            "lbct,lbcd->btd",
            pick_low,
            values.reshape(EXP_DEV, ways, capacity, width),
            preferred_element_type=F32,
        ).astype(LOW)

    expert_grads = dispatch(pick_low, grad_ring.finish())
    expert_rows = dispatch(pick_low, mlp_ring.finish())
    activation, gate_pre_grad, up_pre_grad, pair_grads, weighted, slot_grad = expert_pass(
        jnp.stack([my_expert, my_shard]).astype(jnp.int32),
        expert_rows,
        expert_grads,
        weight_router,
        weights_gate,
        weights_up,
        weights_down,
    )

    def weight_grad(spec, left, right):
        return jnp.einsum(spec, left, right, preferred_element_type=F32).astype(LOW)

    def expert_sum(grad):
        return lax.psum_scatter(grad, "shard", scatter_dimension=1, tiled=True)

    def weight_grad_sum(spec, left, right):
        return expert_sum(weight_grad(spec, left, right))

    grad_down = weight_grad("erf,erd->efd", activation, pair_grads)
    (back_gate, back_up), grad_down = tie((gate_pre_grad, up_pre_grad), grad_down)
    grad_down = expert_sum(grad_down)
    weighted, _ = tie(weighted, back_up)
    mixed_sum = combine(weighted)
    mixed_ring = RingScatter(lambda j: mixed_sum[j], ways)
    mixed_ring.step()
    rows_sum = mixed_ring.tie(combine(row_grads(back_gate, back_up, weights_gate, weights_up)))
    rows_ring = RingScatter(lambda j: rows_sum[j], ways)
    rows_ring.step()
    gate_pre_grad = rows_ring.tie(gate_pre_grad)
    grad_gate = weight_grad_sum("erd,erf->edf", expert_rows, gate_pre_grad)
    rows_ring.step()
    slot_grad = rows_ring.tie(slot_grad)
    slot_grad = slot_grad.reshape(EXP_DEV, ways, capacity, 1)
    token_grad = jnp.sum(jnp.where(pick, slot_grad, 0.0), axis=2).transpose(1, 0, 2)
    back_order = (my_place - jnp.array(ring_order_inverse(ways), jnp.int32)) % ways
    token_grad = jnp.take(token_grad, back_order, axis=0)
    router_grad = lax.all_to_all(token_grad, "expert", split_axis=0, concat_axis=0, tiled=True)
    router_grad = router_grad.reshape(ways * EXP_DEV, tokens).T
    rows_ring.step()
    router_grad = rows_ring.tie(router_grad)
    mlp_grad = rows_ring.finish()
    logit_grad = (
        router * (router_grad - jnp.sum(router * router_grad, axis=-1, keepdims=True))
    ).astype(LOW)
    grad_router = dot_first(mlp_in, logit_grad)
    mlp_in_grad = mlp_grad + dot_last(logit_grad, weight_router)
    hidden_part, gain_mlp_grad = rms_back(hidden, inverse_hidden, gain_mlp, mlp_in_grad)
    hidden_grad = out_grad + hidden_part
    hidden_low = hidden_grad.astype(LOW)
    mixed_ring.state, hidden_low = tie(mixed_ring.state, hidden_low)
    attn_ring = ShardGather(hidden_low, shards)
    attn_ring.hop()
    mixed_ring.step()
    attn_ring.held = mixed_ring.tie(attn_ring.held)
    mixed_ring.step()
    up_pre_grad, _ = tie(up_pre_grad, attn_ring.held)
    grad_up = weight_grad_sum("erd,erf->edf", expert_rows, up_pre_grad)
    attn_grad = attn_ring.whole(my_shard)
    grad_output = dot_first(attended, attn_grad).astype(LOW).reshape(width, part)

    def piece_of(whole):
        size = whole.shape[0] // ways
        return lambda j: lax.dynamic_slice_in_dim(whole, ring[j] * size, size, 0)

    attended_grad = dot_last(attn_grad, weight_output).astype(LOW)

    query_grad, key_grad, value_grad = attend_back(
        query, key, value, attended_grad, log_total, cosine, sine, segments
    )
    query_grad = mixed_ring.tie(query_grad)
    mixed_ring.step()
    inner = jnp.stack(
        [
            jnp.sum(query_raw * gain_query * query_grad, axis=-1),
            jnp.sum(key_raw * gain_key * key_grad, axis=-1),
        ]
    )
    inner, grad_down = tie(inner, grad_down)
    grad_down = grad_down.astype(F32)
    inner = tile_sum(inner) / width
    gain_query_grad = jnp.sum(query_grad * query_raw * inverse_query, axis=0)
    gain_key_grad = jnp.sum(key_grad * key_raw * inverse_key, axis=0)
    query_raw_grad = inverse_query * gain_query * query_grad - query_raw * (
        inverse_query**3 * inner[0][:, None]
    )
    key_raw_grad = inverse_key * gain_key * key_grad - key_raw * (
        inverse_key**3 * inner[1][:, None]
    )
    three_grad = jnp.concatenate(
        [query_raw_grad.astype(LOW), key_raw_grad.astype(LOW), value_grad], axis=1
    )
    normed_grad = dot_last(three_grad, weight_three).astype(LOW)
    normed_sum = ShardScatter(shard_pieces(normed_grad, shards, my_shard), shards)
    while 2 * normed_sum.distance < shards:
        normed_sum.hop()
    grad_three = dot_first(normed_all, three_grad).astype(LOW)

    grad_three = mixed_ring.tie(grad_three)
    output = hidden + mixed_ring.finish()
    three_piece, output_piece = piece_of(grad_three), piece_of(grad_output)
    three_ring = RingScatter(
        lambda j: jnp.concatenate([three_piece(j), output_piece(j)], axis=1), ways
    )
    for step in range(ways // 2):
        three_ring.step()
        if step == ways // 2 - 2:
            three_ring.state, grad_gate = tie(three_ring.state, grad_gate)
            grad_gate = grad_gate.astype(F32)
            normed_sum.hop(three_ring.state)
    rows_part, gain_attn_grad = rms_back(rows, inverse_rows, gain_attn, normed_sum.finish())
    input_grad = hidden_grad + rows_part
    joined = three_ring.finish().astype(LOW)
    grad_three = joined[:, : 3 * part]
    grad_output = joined[:, 3 * part :].reshape(own_rows, width)
    grad_output = lax.ppermute(grad_output, both, from_slice).astype(F32)
    grad_up, _ = tie(grad_up, grad_three)
    grad_up = grad_up.astype(F32)
    grad_three = lax.all_to_all(
        grad_three.reshape(shards, own_rows, 3 * part),
        "shard",
        split_axis=0,
        concat_axis=0,
        tiled=True,
    )
    grad_three = grad_three.reshape(shards, own_rows, 3, part).transpose(2, 1, 0, 3)
    grad_three = grad_three.reshape(3, own_rows, width).astype(F32)

    zeros = jnp.zeros((width,), F32)

    def placed(piece):
        return lax.dynamic_update_slice_in_dim(zeros, piece, my_shard * part, 0)

    gain_grads = jnp.stack(
        [gain_attn_grad, placed(gain_query_grad), placed(gain_key_grad), gain_mlp_grad], axis=1
    )
    small_grad = jnp.concatenate([gain_grads, grad_router], axis=1)
    small_grad = lax.all_to_all(
        small_grad.reshape(devices, own_rows, -1), both, split_axis=0, concat_axis=0, tiled=True
    )
    small_grad = jnp.sum(small_grad, axis=0)
    return (
        output[None],
        input_grad[None],
        small_grad[:, :4].T,
        grad_three[0],
        grad_three[1],
        grad_three[2],
        grad_output,
        small_grad[:, 4:],
        grad_gate,
        grad_up,
        grad_down,
    )


def solution(mesh):
    tokens = P("expert", "shard", None)
    flat = P(("expert", "shard"), None)
    return jax.shard_map(
        per_device,
        mesh=mesh,
        in_specs=(
            tokens,
            P("expert", None),
            tokens,
            P(None, ("expert", "shard")),
            flat,
            flat,
            flat,
            flat,
            flat,
            tokens,
            tokens,
            tokens,
            tokens,
        ),
        out_specs=(
            tokens,
            tokens,
            P(None, ("expert", "shard")),
            flat,
            flat,
            flat,
            flat,
            flat,
            tokens,
            tokens,
            tokens,
        ),
        check_vma=False,
    )
```
